512 devices in a mesh: tok: 4 (over x_hi, core), qry: 8 (over x_lo, y), eig: 16 (over z).
Axes of the slice: x: 4 (x_hi: 2, x_lo: 2; x = x_hi * 2 + x_lo), y: 4, z: 16, core: 2. Of those that a mesh axis runs over, the one named last changes fastest.
Arguments:
- train_acts: bfloat16 [3072, 2560], P('tok', 'qry'), may hold values from -6 to 6
- train_grads: bfloat16 [3072, 6912], P('tok', 'qry'), may hold values from -6 to 6
- query_acts: bfloat16 [16, 32, 2560], P(None, None, 'qry'), may hold values from -6 to 6
- query_grads: bfloat16 [16, 32, 6912], P(None, None, 'qry'), may hold values from -6 to 6
- in_basis: bfloat16 [2560, 2560], P('qry', 'eig'), may hold values from -0.125 to 0.125
- out_basis: bfloat16 [6912, 6912], P('qry', 'eig'), may hold values from -0.078125 to 0.078125
- eigenvalues: float32 [6912, 2560], P('eig', 'tok'), may hold values from 0.01 to 324, as said below
Outputs:
- scores: float32 [3072, 16], P('tok', 'qry')
The draws below stay inside these ranges and needn't reach their ends.
Inputs may be any that keep to these rules, and one draw needn't show every extreme that they name: `eigenvalues`: every entry is positive.
All inputs are finite; a program needn't handle non-finite values.
Results may differ from the reference program's by a relative error of at most 0.0048.
Values may be sent and summed in bfloat16 or wider, within the bound.
A program may use at most 64 MiB of HBM per device.

```python
import math
import jax
import jax.numpy as jnp
from jax import lax

DIN = 2560
DOUT = 6912
LQ = 32
TOKENS = 3072
QUERIES = 16


def draw_eigenvalues(key, part):
    key = jax.random.fold_in(key, 7)
    base_key = jax.random.fold_in(key, 1)
    level_key = jax.random.fold_in(key, 2)
    rows = jnp.arange(DOUT, dtype=jnp.float32)[:, None] / DOUT
    cols = jnp.arange(DIN, dtype=jnp.float32)[None, :] / DIN
    row_block = jnp.arange(DOUT, dtype=jnp.int32) * 16 // DOUT
    col_block = jnp.arange(DIN, dtype=jnp.int32) * 4 // DIN
    lower, upper, trend = (math.log(0.08), math.log(2.0), 3.0)
    base = jnp.exp(jax.random.uniform(base_key, (DOUT, DIN), jnp.float32, lower, upper))
    levels = jnp.exp(jax.random.uniform(level_key, (16, 4), jnp.float32, -2.0, 2.0))
    block_level = levels[row_block[:, None], col_block[None, :]]
    values = base * jnp.power(trend, rows) * jnp.power(trend, cols) * block_level
    return jnp.clip(values, 0.01, 324.0)


def block_levels(rng, extent, split, least, high):
    gain = 1.0
    for axis_at, shards_of in split:
        steps = jax.random.uniform(jax.random.fold_in(jax.random.fold_in(rng, 6), axis_at), (shards_of,), jnp.float32, least / len(split), high / len(split))
        gain = gain * jnp.repeat(jnp.exp(steps), extent[axis_at] // shards_of).reshape((-1,) + (1,) * (len(extent) - 1 - axis_at))
    return gain


def scatter_about(own_key, shape, spread, limit, split=(), kind=jnp.bfloat16):
    entries = jax.random.normal(own_key, shape, jnp.float32) * spread
    if len(split) > 0:
        entries = block_levels(own_key, shape, split, -0.22, 0.18) * entries
    return jnp.clip(entries, min=-limit, max=limit).astype(kind)


def setup_inputs(seed: int = 0) -> dict:
    key_of = jax.random.split(jax.random.key(seed), 8)
    train_acts = scatter_about(key_of[0], (TOKENS, DIN), 1.0, 6.0, ((0, 4), (1, 8)))
    train_grads = scatter_about(key_of[1], (TOKENS, DOUT), 1.0, 6.0, ((0, 4), (1, 8)))
    query_acts = scatter_about(key_of[2], (QUERIES, LQ, DIN), 1.0, 6.0, ((2, 8),))
    query_grads = scatter_about(key_of[3], (QUERIES, LQ, DOUT), 1.0, 6.0, ((2, 8),))
    in_basis = scatter_about(key_of[4], (DIN, DIN), DIN ** -0.5, 0.125, ((0, 8), (1, 16)))
    out_basis = scatter_about(key_of[5], (DOUT, DOUT), DOUT ** -0.5, 0.078125, ((0, 8), (1, 16)))
    eigenvalues = draw_eigenvalues(jax.random.fold_in(key_of[7], 71), 0)
    return dict(train_acts=train_acts, train_grads=train_grads, query_acts=query_acts, query_grads=query_grads, in_basis=in_basis, out_basis=out_basis, eigenvalues=eigenvalues)


def reference(train_acts, train_grads, query_acts, query_grads, in_basis, out_basis, eigenvalues):
    act_proj = jnp.dot(train_acts, in_basis, preferred_element_type=jnp.float32).astype(jnp.bfloat16)
    grad_proj = jnp.dot(train_grads, out_basis, preferred_element_type=jnp.float32).astype(jnp.bfloat16)
    damping = 0.1 * jnp.mean(eigenvalues)
    shifted = eigenvalues + damping
    factor = 1.0 / jnp.sqrt(jnp.float32(LQ * DOUT * DIN))

    def one_query(pair):
        query_act, query_grad = pair
        query_out = jnp.dot(query_grad, out_basis, preferred_element_type=jnp.float32).astype(jnp.bfloat16)
        query_in = jnp.dot(query_act, in_basis, preferred_element_type=jnp.float32).astype(jnp.bfloat16)
        outer = jnp.dot(query_out.T, query_in, preferred_element_type=jnp.float32)
        panel = (outer / shifted).astype(jnp.bfloat16)
        weighted = lax.dot_general(act_proj, panel, (((1,), (1,)), ((), ())), preferred_element_type=jnp.float32)
        return lax.optimization_barrier(jnp.sum(weighted * grad_proj, axis=1)) * factor
    per_query = lax.map(one_query, (query_acts, query_grads))
    return per_query.T
```

```python
import functools

import jax
import jax.numpy as jnp
from jax import lax
from jax.experimental import pallas as pl
from jax.experimental.pallas import tpu as pltpu
from jax.sharding import PartitionSpec as P

DIN = 2560
DOUT = 6912
LQ = 32

MESH = pl.DeviceIdType.MESH
F32 = jnp.float32
BF16 = jnp.bfloat16

NT = 4
NF = 8
NZ = 16
ROWS = 768
SUB = 96
FI = 320
FO = 864
EI = 160
EO = 432
HALF = 1280
QROWS = 80
QP = 640
CHUNK = 256

NT_DIMS = (((1,), (1,)), ((), ()))


def dot(a, b):
    return jnp.dot(a, b, preferred_element_type=F32)


def rcopy(src, dst, send_sem, recv_sem, dev):
    return pltpu.make_async_remote_copy(
        src_ref=src,
        dst_ref=dst,
        send_sem=send_sem,
        recv_sem=recv_sem,
        device_id=dev,
        device_id_type=MESH,
    )


def kernel(
    ta_h, tg_h, qa_h, qg_h, v_h, u_h, ev_h,
    out_ref,
    ta, tg, qa, qg, v, u, ev,
    qpart, qrecv, qt, apart, arecv, at, gpart, grecv, gown, gt_own, gt,
    evb, evh, rinv, za, zq, pan, tsum, trecv, zsum, zrecv,
    stage, srecv, fsum, frecv,
    in_sem,
    q_s, q_r, qg_s, qg_r, a_s, a_r, g_s, g_r,
    sib_s, sib_r, ga_s, ga_r, ev_s, ev_r, t_s, t_r, zs_s, zs_r,
    rq_s, rq_r, ra_s, ra_r, pa_s, pa_r, sc_s, sc_r, fz_s, fz_r,
):
    tok = lax.axis_index("tok")
    qry = lax.axis_index("qry")
    z = lax.axis_index("eig")
    c = tok % 2
    xh = tok // 2
    xl = qry // 4
    y = qry % 4
    sib = (xh * 2 + 1 - c, qry, z)
    pqry = (1 - xl) * 4 + y
    slot = z % 8
    owner = z // 8 == c

    loads = []
    for n, (src, dst) in enumerate(
        (
            (qg_h.at[pl.ds(tok * 128, 128)], qg),
            (u_h, u),
            (qa_h.at[pl.ds(tok * 128, 128)], qa),
            (v_h, v),
            (ta_h, ta),
            (ev_h, ev),
            (tg_h, tg),
        )
    ):
        load = pltpu.make_async_copy(src, dst, in_sem.at[n])
        load.start()
        loads.append(load)

    barrier = pltpu.get_barrier_semaphore()
    for dt in range(NT):
        for df in range(NF):
            if dt or df:
                pl.semaphore_signal(
                    barrier,
                    inc=1,
                    device_id=((tok + dt) % NT, (qry + df) % NF, z),
                    device_id_type=MESH,
                )
    for dz in range(1, NZ):
        pl.semaphore_signal(
            barrier, inc=1, device_id=(tok, qry, (z + dz) % NZ), device_id_type=MESH
        )

    for n in range(4):
        loads[n].wait()
    qpart[0:EO, :] = dot(qg[...], u[...]).T
    qpart[EO : EO + EI, :] = dot(qa[...], v[...]).T
    qpart[EO + EI :, :] = jnp.zeros((QP - EO - EI, 128), F32)

    pl.semaphore_wait(barrier, NT * NF - 1 + NZ - 1)

    def q_copy(k):
        to = (qry + k) % NF
        return rcopy(
            qpart.at[pl.ds(pl.multiple_of(to * QROWS, 16), QROWS)],
            qrecv.at[k],
            q_s.at[k],
            q_r.at[k],
            (tok, to, z),
        )

    for k in range(1, NF):
        q_copy(k).start()

    loads[4].wait()
    apart[...] = dot(ta[...], v[...]).astype(BF16)

    def a_copy(k):
        to = (qry + k) % NF
        return rcopy(
            apart.at[pl.ds(pl.multiple_of(to * SUB, 16), SUB)],
            arecv.at[k],
            a_s.at[k],
            a_r.at[k],
            (tok, to, z),
        )

    for k in range(1, NF):
        a_copy(k).start()

    loads[5].wait()
    evals = ev[...]
    evb[...] = evals.astype(BF16)
    rows8 = jnp.sum(evals.reshape(EO // 8, 8, 640), axis=0)
    tsum[...] = sum(rows8[:, 128 * n : 128 * n + 128] for n in range(5))

    def t_copy(dt):
        return rcopy(
            tsum, trecv.at[dt], t_s.at[dt], t_r.at[dt], ((tok + dt) % NT, qry, z)
        )

    for dt in range(1, NT):
        t_copy(dt).start()

    def ev_far():
        return rcopy(
            evb, evh.at[c], ev_s.at[0], ev_r.at[c], ((1 - xh) * 2 + xh, pqry, z)
        )

    def ev_near():
        return rcopy(evb, evh.at[c], ev_s.at[1], ev_r.at[c], sib)

    ev_far().start()

    @pl.when(c == xh)
    def _():
        evh[c] = evb[...]

    @pl.when(c != xh)
    def _():
        ev_near().start()

    for k in range(1, NF):
        q_copy(k).wait_recv()
    mine = qpart[pl.ds(pl.multiple_of(qry * QROWS, 16), QROWS), :]
    for k in range(1, NF):
        mine = mine + qrecv[k]
    qt[c, pl.ds(pl.multiple_of(qry * QROWS, 16), QROWS), :] = mine.astype(BF16)

    def qg_copy(dc, k):
        block = qt.at[c, pl.ds(pl.multiple_of(qry * QROWS, 16), QROWS)]
        return rcopy(
            block,
            block,
            qg_s.at[dc, k],
            qg_r.at[dc, k],
            (xh * 2 + (c + dc) % 2, (qry + k) % NF, z),
        )

    def qg_arrival(dc, k):
        frm = (qry - k + NF) % NF
        block = qt.at[
            (c + dc) % 2, pl.ds(pl.multiple_of(frm * QROWS, 16), QROWS)
        ]
        return rcopy(block, block, qg_s.at[dc, k], qg_r.at[dc, k], sib)

    peers = [(dc, k) for k in range(NF) for dc in range(2) if dc or k]
    for dc, k in peers:
        qg_copy(dc, k).start()

    for k in range(1, NF):
        a_copy(k).wait_recv()
    asum = apart[pl.ds(pl.multiple_of(qry * SUB, 16), SUB), :].astype(F32)
    for k in range(1, NF):
        asum = asum + arecv[k].astype(F32)
    asum = jnp.concatenate([asum, jnp.zeros((128 - SUB, EI), F32)], axis=0)
    at[...] = asum.T.astype(BF16)

    my_rows = pl.ds(pl.multiple_of(slot * EI, 16), EI)
    my_lanes = pl.ds(pl.multiple_of(c * 128, 128), 128)
    sib_lanes = pl.ds(pl.multiple_of((1 - c) * 128, 128), 128)

    def sib_copy():
        return rcopy(at, za.at[my_rows, my_lanes], sib_s.at[0], sib_r.at[0], sib)

    @pl.when(owner)
    def _():
        za[my_rows, my_lanes] = at[...]

    @pl.when(jnp.logical_not(owner))
    def _():
        sib_copy().start()

    for dt in range(1, NT):
        t_copy(dt).wait_recv()
    zsum[...] = tsum[...] + trecv[1] + trecv[2] + trecv[3]

    def zs_copy(dz):
        return rcopy(
            zsum, zrecv.at[dz], zs_s.at[dz], zs_r.at[dz], (tok, qry, (z + dz) % NZ)
        )

    for dz in range(1, NZ):
        zs_copy(dz).start()

    up = (tok, qry, (z + 1) % NZ)
    down = (tok, qry, (z + NZ - 1) % NZ)

    def blk(buf, s):
        rows = pl.ds(pl.multiple_of(s * EI, 16), EI)
        return buf.at[rows, pl.ds(0, 256)]

    def hop(buf, sends, recvs, s, way):
        return rcopy(
            blk(buf, s), blk(buf, s), sends.at[way, s], recvs.at[s], (up, down)[way]
        )

    def ring_open(buf, sends, recvs):
        hop(buf, sends, recvs, slot, 0).start()
        hop(buf, sends, recvs, slot, 1).start()

    def ring_step(buf, sends, recvs, s, after=None):
        for way, last in ((0, 8), (1, 7)):
            if s > last:
                continue
            origin = (z + NZ - s) % NZ if way == 0 else (z + s) % NZ

            @pl.when(origin // 8 == c)
            def _():
                hop(buf, sends, recvs, origin % 8, way).wait_recv()
                if s < last:
                    hop(buf, sends, recvs, origin % 8, way).start()
                if after is not None:
                    after(origin % 8)

    def ring_close(buf, sends, recvs):
        for s in range(8):
            for way, last in ((0, 8), (1, 7)):
                if s >= last:
                    continue
                origin = (z + NZ - s) % NZ if way == 0 else (z + s) % NZ

                @pl.when(origin // 8 == c)
                def _():
                    hop(buf, sends, recvs, origin % 8, way).wait_send()

    def pa_copy(s):
        rows = pl.ds(pl.multiple_of(s * EI, 16), EI)
        return rcopy(
            za.at[rows, pl.ds(0, 256)],
            za.at[rows, pl.ds(256, 256)],
            pa_s.at[s],
            pa_r.at[s],
            ((1 - xh) * 2 + c, pqry, z),
        )

    for dc, k in peers:
        qg_arrival(dc, k).wait_recv()

    @pl.when(owner)
    def _():
        for n in range(2):
            zq[my_rows, 128 * n : 128 * n + 128] = qt[n, EO : EO + EI, :]
        ring_open(zq, rq_s, rq_r)
        rcopy(
            at, za.at[my_rows, sib_lanes], sib_s.at[0], sib_r.at[0], sib
        ).wait_recv()
        ring_open(za, ra_s, ra_r)
        pa_copy(slot).start()

    loads[6].wait()

    def g_copy(k):
        return rcopy(
            gpart.at[k], grecv.at[k], g_s.at[k], g_r.at[k], (tok, (qry + k) % NF, z)
        )

    for k in range(1, NF + 1):
        to = (qry + k) % NF
        rows = pl.ds(pl.multiple_of(to * SUB, 16), SUB)
        part = dot(tg[rows, :], u[...])
        if k < NF:
            gpart[k] = part.astype(BF16)
            g_copy(k).start()
        else:
            gown[...] = part
        ring_step(zq, rq_s, rq_r, k)

    for dz in range(1, NZ):
        zs_copy(dz).wait_recv()
    total = zsum[...]
    for dz in range(1, NZ):
        total = total + zrecv[dz]
    damping = 0.1 * (jnp.sum(total) / (DIN * DOUT))

    ev_other = rcopy(evb, evh.at[1 - c], ev_s.at[0], ev_r.at[1 - c], sib)
    ev_other.wait_recv()

    @pl.when(c != xh)
    def _():
        rcopy(evb, evh.at[c], ev_s.at[0], ev_r.at[c], sib).wait_recv()

    for n in range(2):
        rinv[:, 640 * n : 640 * n + 640] = 1.0 / (evh[n].astype(F32) + damping)

    qot = jnp.concatenate([qt[0, 0:EO, :], qt[1, 0:EO, :]], axis=1)
    lane = lax.broadcasted_iota(jnp.int32, (EO, 256), 1) // LQ

    def panel(q, carry):
        left = jnp.where(lane == q, qot, jnp.zeros_like(qot))
        for n in range(HALF // CHUNK):
            cols = slice(CHUNK * n, CHUNK * n + CHUNK)
            outer = lax.dot_general(
                left, zq[cols, :], NT_DIMS, preferred_element_type=F32
            )
            pan[q, :, cols] = (outer * rinv[:, cols]).astype(BF16)
        return carry

    for s in range(1, 9):
        ring_step(za, ra_s, ra_r, s, lambda o: pa_copy(o).start())
        panel(s - 1, 0)

    for k in range(1, NF):
        g_copy(k).wait_recv()
    gsum = gown[...]
    for k in range(1, NF):
        gsum = gsum + grecv[k].astype(F32)
    gsum = jnp.concatenate([gsum, jnp.zeros((128 - SUB, EO), F32)], axis=0)
    gt_own[...] = gsum.T.astype(BF16)
    gt[:, my_lanes] = gt_own[...]
    far_lanes = pl.ds(pl.multiple_of(256 + c * 128, 128), 128)

    ga_copies = [
        rcopy(gt_own, gt.at[:, my_lanes], ga_s.at[0], ga_r.at[0], sib),
        rcopy(
            gt_own, gt.at[:, far_lanes], ga_s.at[1], ga_r.at[1 + c],
            ((1 - xh) * 2, pqry, z),
        ),
        rcopy(
            gt_own, gt.at[:, far_lanes], ga_s.at[2], ga_r.at[1 + c],
            ((1 - xh) * 2 + 1, pqry, z),
        ),
    ]
    for copy in ga_copies:
        copy.start()

    for s in range(8):
        pa_arrival = rcopy(
            za.at[pl.ds(s * EI, EI), pl.ds(0, 256)],
            za.at[pl.ds(s * EI, EI), pl.ds(256, 256)],
            pa_s.at[s],
            pa_r.at[s],
            sib,
        )
        pa_arrival.wait_recv()
    rcopy(gt_own, gt.at[:, sib_lanes], ga_s.at[0], ga_r.at[0], sib).wait_recv()
    for n in range(2):
        lanes = pl.ds(256 + 128 * n, 128)
        rcopy(gt_own, gt.at[:, lanes], ga_s.at[1], ga_r.at[1 + n], sib).wait_recv()

    for q in range(8):
        weighted = dot(pan[q], za[...])
        row = jnp.sum(weighted * gt[...].astype(F32), axis=0, keepdims=True)
        for g in range(4):
            stage[q // 2, g, q % 2 : q % 2 + 1, :] = row[:, 128 * g : 128 * g + 128]

    def sc_copy(k, g):
        if g < 2:
            to_tok, frm = xh * 2 + g, qry
        else:
            to_tok, frm = (1 - xh) * 2 + g - 2, pqry
        return (
            rcopy(
                stage.at[k, g],
                srecv.at[c, frm],
                sc_s.at[k, g],
                sc_r.at[c, frm],
                (to_tok, xh * 4 + k, z),
            ),
            (to_tok == tok) & (xh * 4 + k == qry),
        )

    for k in range(4):
        for g in range(4):
            copy, here = sc_copy(k, g)
            if g < 2:

                @pl.when(here)
                def _():
                    srecv[c, qry] = stage[k, g]

                @pl.when(jnp.logical_not(here))
                def _():
                    copy.start()

            else:
                copy.start()

    for n in range(2):
        for f in range(NF):

            @pl.when(jnp.logical_not((c == n) & (qry == f) & (xh == xl)))
            def _():
                rcopy(
                    stage.at[0, 0], srecv.at[n, f], sc_s.at[0, 0], sc_r.at[n, f], sib
                ).wait_recv()

    factor = 1.0 / jnp.sqrt(F32(LQ * DOUT * DIN))
    for f in range(NF):
        fsum[2 * f : 2 * f + 2, :] = (srecv[0, f, 0:2, :] + srecv[1, f, 0:2, :]) * factor

    def fz_copy(dz):
        return rcopy(
            fsum, frecv.at[dz], fz_s.at[dz], fz_r.at[dz], (tok, qry, (z + dz) % NZ)
        )

    for dz in range(1, NZ):
        fz_copy(dz).start()
    for dz in range(1, NZ):
        fz_copy(dz).wait_recv()
    scores = fsum[...]
    for dz in range(1, NZ):
        scores = scores + frecv[dz]
    out_ref[...] = scores

    for k in range(1, NF):
        q_copy(k).wait_send()
        a_copy(k).wait_send()
        g_copy(k).wait_send()
    for dt in range(1, NT):
        t_copy(dt).wait_send()
    ev_far().wait_send()

    @pl.when(c != xh)
    def _():
        ev_near().wait_send()

    for dc, k in peers:
        qg_copy(dc, k).wait_send()

    @pl.when(jnp.logical_not(owner))
    def _():
        sib_copy().wait_send()

    for dz in range(1, NZ):
        zs_copy(dz).wait_send()
        fz_copy(dz).wait_send()
    ring_close(zq, rq_s, rq_r)
    ring_close(za, ra_s, ra_r)
    for s in range(8):
        pa_copy(s).wait_send()
    for copy in ga_copies:
        copy.wait_send()
    for k in range(4):
        for g in range(4):
            copy, here = sc_copy(k, g)
            if g < 2:

                @pl.when(jnp.logical_not(here))
                def _():
                    copy.wait_send()

            else:
                copy.wait_send()


def shards(train_acts, train_grads, query_acts, query_grads, in_basis, out_basis, eigenvalues):
    dma = pltpu.SemaphoreType.DMA
    vm = pltpu.VMEM
    out = pl.pallas_call(
        kernel,
        out_shape=jax.ShapeDtypeStruct((16, 128), F32),
        in_specs=[pl.BlockSpec(memory_space=pl.ANY)] * 7,
        out_specs=pl.BlockSpec(memory_space=pltpu.VMEM),
        scratch_shapes=[
            vm((ROWS, FI), BF16), vm((ROWS, FO), BF16), vm((128, FI), BF16),
            vm((128, FO), BF16), vm((FI, EI), BF16), vm((FO, EO), BF16),
            vm((EO, 640), F32),
            vm((QP, 128), F32), vm((NF, QROWS, 128), F32), vm((2, QP, 128), BF16),
            vm((ROWS, EI), BF16), vm((NF, SUB, EI), BF16), vm((EI, 128), BF16),
            vm((NF, SUB, EO), BF16), vm((NF, SUB, EO), BF16), vm((SUB, EO), F32),
            vm((EO, 128), BF16), vm((EO, 512), BF16),
            vm((EO, 640), BF16), vm((2, EO, 640), BF16), vm((EO, HALF), F32),
            vm((HALF, 512), BF16), vm((HALF, 256), BF16), vm((8, EO, HALF), BF16),
            vm((8, 128), F32), vm((NT, 8, 128), F32),
            vm((8, 128), F32), vm((NZ, 8, 128), F32),
            vm((4, 4, 8, 128), F32), vm((2, NF, 8, 128), F32),
            vm((16, 128), F32), vm((NZ, 16, 128), F32),
            dma((7,)),
            dma((NF,)), dma((NF,)), dma((2, NF)), dma((2, NF)),
            dma((NF,)), dma((NF,)), dma((NF,)), dma((NF,)),
            dma((1,)), dma((1,)), dma((3,)), dma((3,)),
            dma((2,)), dma((2,)), dma((NT,)), dma((NT,)), dma((NZ,)), dma((NZ,)),
            dma((2, 8)), dma((8,)), dma((2, 8)), dma((8,)),
            dma((8,)), dma((8,)), dma((4, 4)), dma((2, NF)), dma((NZ,)), dma((NZ,)),
        ],
        compiler_params=pltpu.CompilerParams(
            collective_id=0, has_side_effects=True, vmem_limit_bytes=56 * 1024 * 1024
        ),
    )(
        train_acts,
        train_grads,
        query_acts.reshape(16 * LQ, FI),
        query_grads.reshape(16 * LQ, FO),
        in_basis,
        out_basis,
        eigenvalues,
    )
    return out.reshape(NF, 2, 128)[:, :, :SUB].transpose(0, 2, 1).reshape(ROWS, 2)


def solution(mesh):
    placed = (
        P("tok", "qry"),
        P("tok", "qry"),
        P(None, None, "qry"),
        P(None, None, "qry"),
        P("qry", "eig"),
        P("qry", "eig"),
        P("eig", "tok"),
    )
    return jax.shard_map(
        shards, mesh=mesh, in_specs=placed, out_specs=P("tok", "qry"), check_vma=False
    )
```

```python
import functools

import jax
import jax.numpy as jnp
from jax import lax
from jax.experimental import pallas as pl
from jax.experimental.pallas import tpu as pltpu
from jax.sharding import PartitionSpec as P

DIN = 2560
DOUT = 6912
LQ = 32

MESH = pl.DeviceIdType.MESH
F32 = jnp.float32
BF16 = jnp.bfloat16

NT = 4
NF = 8
NZ = 16
ROWS = 768
SUB = 96
FI = 320
FO = 864
EI = 160
EO = 432
HALF = 1280
QROWS = 80
QP = 640
CHUNK = 256

TREE = {0: (3, -3, 1, -1), 3: (3, 1, -1), -3: (-3, -1, 1), 6: (2, 1, -1), -6: (-1, 1)}
NEAR = (1, -1, 2, -2, 3, -3)

NT_DIMS = (((1,), (1,)), ((), ()))


def dot(a, b):
    return jnp.dot(a, b, preferred_element_type=F32)


def dot_nt(a, b):
    return lax.dot_general(a, b, NT_DIMS, preferred_element_type=F32)


def lanes_of(whole, f):
    part = whole[:, SUB * f : SUB * f + SUB]
    return jnp.concatenate(
        [part, jnp.zeros((part.shape[0], 128 - SUB), part.dtype)], axis=1
    )


def rcopy(src, dst, send_sem, recv_sem, dev):
    return pltpu.make_async_remote_copy(
        src_ref=src,
        dst_ref=dst,
        send_sem=send_sem,
        recv_sem=recv_sem,
        device_id=dev,
        device_id_type=MESH,
    )


def kernel(
    ta_h, tg_h, qa_h, qg_h, v_h, u_h, ev_h,
    out_ref,
    ta, tg, qa, qg, v, u, ev,
    qpart, qrecv, qt, apart, arecv, at, gpart, grecv, gt_own, gt,
    evb, evh, rinv, za, zq, pan, tsum, trecv, zsum, zrecv,
    stage, srecv, fsum, frecv,
    in_sem,
    q_s, q_r, qg_s, qg_r, a_s, a_r, g_s, g_r,
    sib_s, sib_r, ga_s, ga_r, ev_s, ev_r, t_s, t_r, zs_s, zs_r,
    rq_s, rq_r, ra_s, ra_r, pa_s, pa_r, sc_s, sc_r, fz_s, fz_r,
):
    tok = lax.axis_index("tok")
    qry = lax.axis_index("qry")
    z = lax.axis_index("eig")
    c = tok % 2
    xh = tok // 2
    xl = qry // 4
    y = qry % 4
    sib = (xh * 2 + 1 - c, qry, z)
    pqry = (1 - xl) * 4 + y
    slot = z % 8
    owner = z // 8 == c

    loads = []
    for n, (src, dst) in enumerate(
        (
            (qg_h.at[pl.ds(tok * 128, 128)], qg),
            (u_h, u),
            (qa_h.at[pl.ds(tok * 128, 128)], qa),
            (v_h, v),
            (ta_h, ta),
            (ev_h, ev),
            (tg_h, tg),
        )
    ):
        load = pltpu.make_async_copy(src, dst, in_sem.at[n])
        load.start()
        loads.append(load)

    barrier = pltpu.get_barrier_semaphore()
    for dt in range(NT):
        for df in range(NF):
            if dt or df:
                pl.semaphore_signal(
                    barrier,
                    inc=1,
                    device_id=((tok + dt) % NT, (qry + df) % NF, z),
                    device_id_type=MESH,
                )
    for dz in NEAR:
        pl.semaphore_signal(
            barrier,
            inc=1,
            device_id=(tok, qry, (z + dz + NZ) % NZ),
            device_id_type=MESH,
        )

    for n in range(4):
        loads[n].wait()
    qpart[0:EO, :] = dot_nt(u[...], qg[...])
    qpart[EO : EO + EI, :] = dot_nt(v[...], qa[...])
    qpart[EO + EI :, :] = jnp.zeros((QP - EO - EI, 128), F32)

    pl.semaphore_wait(barrier, NT * NF - 1 + len(NEAR))

    def q_copy(k):
        to = (qry + k) % NF
        return rcopy(
            qpart.at[pl.ds(pl.multiple_of(to * QROWS, 16), QROWS)],
            qrecv.at[k],
            q_s.at[k],
            q_r.at[k],
            (tok, to, z),
        )

    for k in range(1, NF):
        q_copy(k).start()

    loads[4].wait()
    a_all = dot(v[...], ta[...]).astype(BF16)
    for f in range(NF):
        apart[f] = lanes_of(a_all, f)

    def a_copy(k):
        to = (qry + k) % NF
        return rcopy(apart.at[to], arecv.at[k], a_s.at[k], a_r.at[k], (tok, to, z))

    for k in range(1, NF):
        a_copy(k).start()

    loads[5].wait()
    evals = ev[...]
    evb[...] = evals.astype(BF16)
    rows8 = jnp.sum(evals.reshape(EO // 8, 8, 640), axis=0)
    tsum[...] = sum(rows8[:, 128 * n : 128 * n + 128] for n in range(5))

    def t_copy(dt):
        return rcopy(
            tsum, trecv.at[dt], t_s.at[dt], t_r.at[dt], ((tok + dt) % NT, qry, z)
        )

    for dt in range(1, NT):
        t_copy(dt).start()

    def ev_far():
        return rcopy(
            evb, evh.at[c], ev_s.at[0], ev_r.at[c], ((1 - xh) * 2 + xh, pqry, z)
        )

    def ev_near():
        return rcopy(evb, evh.at[c], ev_s.at[1], ev_r.at[c], sib)

    ev_far().start()

    @pl.when(c == xh)
    def _():
        evh[c] = evb[...]

    @pl.when(c != xh)
    def _():
        ev_near().start()

    loads[6].wait()
    for half in range(2):
        lanes = slice(384 * half, 384 * half + 384)
        g_all = dot(u[...], tg[:, lanes]).astype(BF16)
        for f in range(4):
            gpart[4 * half + f] = lanes_of(g_all, f)

    for k in range(1, NF):
        q_copy(k).wait_recv()
    mine = qpart[pl.ds(pl.multiple_of(qry * QROWS, 16), QROWS), :]
    for k in range(1, NF):
        mine = mine + qrecv[k]
    qt[c, pl.ds(pl.multiple_of(qry * QROWS, 16), QROWS), :] = mine.astype(BF16)

    def qg_copy(dc, k):
        block = qt.at[c, pl.ds(pl.multiple_of(qry * QROWS, 16), QROWS)]
        return rcopy(
            block,
            block,
            qg_s.at[dc, k],
            qg_r.at[dc, k],
            (xh * 2 + (c + dc) % 2, (qry + k) % NF, z),
        )

    def qg_arrival(dc, k):
        frm = (qry - k + NF) % NF
        block = qt.at[
            (c + dc) % 2, pl.ds(pl.multiple_of(frm * QROWS, 16), QROWS)
        ]
        return rcopy(block, block, qg_s.at[dc, k], qg_r.at[dc, k], sib)

    peers = [(dc, k) for k in range(NF) for dc in range(2) if dc or k]
    for dc, k in peers:
        qg_copy(dc, k).start()

    for k in range(1, NF):
        a_copy(k).wait_recv()
    asum = apart[qry].astype(F32)
    for k in range(1, NF):
        asum = asum + arecv[k].astype(F32)
    for dt in range(1, NT):
        t_copy(dt).wait_recv()
    plane_sum = jnp.sum(tsum[...] + trecv[1] + trecv[2] + trecv[3], keepdims=True)
    high = plane_sum.astype(BF16).astype(F32)
    spot = lax.broadcasted_iota(jnp.int32, (EI, 128), 1)
    asum = jnp.where(spot == SUB, high, asum)
    asum = jnp.where(spot == SUB + 1, plane_sum - high, asum)
    at[...] = asum.astype(BF16)

    my_rows = pl.ds(pl.multiple_of(slot * EI, 16), EI)
    my_lanes = pl.ds(pl.multiple_of(c * 128, 128), 128)
    sib_lanes = pl.ds(pl.multiple_of((1 - c) * 128, 128), 128)

    def sib_copy():
        return rcopy(at, za.at[my_rows, my_lanes], sib_s.at[0], sib_r.at[0], sib)

    @pl.when(owner)
    def _():
        za[my_rows, my_lanes] = at[...]

    @pl.when(jnp.logical_not(owner))
    def _():
        sib_copy().start()

    def blk(buf, s):
        rows = pl.ds(pl.multiple_of(s * EI, 16), EI)
        return buf.at[rows, pl.ds(0, 256)]

    def hop(buf, sends, recvs, s, n, by):
        return rcopy(
            blk(buf, s),
            blk(buf, s),
            sends.at[n, s],
            recvs.at[s],
            (tok, qry, (z + by + NZ) % NZ),
        )

    def gather_open(buf, sends, recvs):
        for n, by in enumerate(TREE[0]):
            hop(buf, sends, recvs, slot, n, by).start()

    def gather_step(buf, sends, recvs, far, after=None):
        origin = (z - far + NZ) % NZ

        @pl.when(origin // 8 == c)
        def _():
            hop(buf, sends, recvs, origin % 8, 0, 1).wait_recv()
            for n, by in enumerate(TREE.get(far, ())):
                hop(buf, sends, recvs, origin % 8, n, by).start()
            if after is not None:
                after(origin % 8)

    def gather_close(buf, sends, recvs):
        for far, on in TREE.items():
            origin = (z - far + NZ) % NZ

            @pl.when(origin // 8 == c)
            def _():
                for n, by in enumerate(on):
                    hop(buf, sends, recvs, origin % 8, n, by).wait_send()

    def pa_copy(s):
        rows = pl.ds(pl.multiple_of(s * EI, 16), EI)
        return rcopy(
            za.at[rows, pl.ds(0, 256)],
            za.at[rows, pl.ds(256, 256)],
            pa_s.at[s],
            pa_r.at[s],
            ((1 - xh) * 2 + c, pqry, z),
        )

    @pl.when(owner)
    def _():
        rcopy(
            at, za.at[my_rows, sib_lanes], sib_s.at[0], sib_r.at[0], sib
        ).wait_recv()
        gather_open(za, ra_s, ra_r)
        pa_copy(slot).start()

    for dc, k in peers:
        qg_arrival(dc, k).wait_recv()

    @pl.when(owner)
    def _():
        for n in range(2):
            zq[my_rows, 128 * n : 128 * n + 128] = qt[n, EO : EO + EI, :]
        gather_open(zq, rq_s, rq_r)

    def g_copy(k):
        return rcopy(
            gpart.at[(qry + k) % NF],
            grecv.at[k],
            g_s.at[k],
            g_r.at[k],
            (tok, (qry + k) % NF, z),
        )

    for k in range(1, NF):
        g_copy(k).start()

    for far in (3, -3, 6, -6):
        gather_step(za, ra_s, ra_r, far, lambda o: pa_copy(o).start())
        gather_step(zq, rq_s, rq_r, far)
    for far in (1, -1, 2, -2, 4, -4, 5, -5, 7, -7, 8):
        gather_step(za, ra_s, ra_r, far, lambda o: pa_copy(o).start())
        gather_step(zq, rq_s, rq_r, far)

    half_sum = jnp.zeros((1, 2), F32)
    for n in range(8):
        half_sum = half_sum + za[EI * n : EI * n + 16, SUB : SUB + 2].astype(F32)[0:1]
    half_sum = jnp.sum(half_sum, keepdims=True)
    zsum[...] = jnp.broadcast_to(half_sum, (8, 128))
    zs_copy = rcopy(zsum, zrecv, zs_s.at[0], zs_r.at[0], sib)
    zs_copy.start()
    zs_copy.wait_recv()
    damping = 0.1 * ((zsum[0:1, 0:1] + zrecv[0:1, 0:1]) / (DIN * DOUT))

    ev_other = rcopy(evb, evh.at[1 - c], ev_s.at[0], ev_r.at[1 - c], sib)
    ev_other.wait_recv()

    @pl.when(c != xh)
    def _():
        rcopy(evb, evh.at[c], ev_s.at[0], ev_r.at[c], sib).wait_recv()

    for n in range(2):
        rinv[:, 640 * n : 640 * n + 640] = 1.0 / (evh[n].astype(F32) + damping)

    qot = jnp.concatenate([qt[0, 0:EO, :], qt[1, 0:EO, :]], axis=1)
    lane = lax.broadcasted_iota(jnp.int32, (EO, 256), 1) // LQ

    def panel(q):
        left = jnp.where(lane == q, qot, jnp.zeros_like(qot))
        for n in range(HALF // CHUNK):
            cols = slice(CHUNK * n, CHUNK * n + CHUNK)
            outer = dot_nt(left, zq[cols, :])
            pan[q, :, cols] = (outer * rinv[:, cols]).astype(BF16)

    for q in range(8):
        panel(q)

    for k in range(1, NF):
        g_copy(k).wait_recv()
    gsum = gpart[qry].astype(F32)
    for k in range(1, NF):
        gsum = gsum + grecv[k].astype(F32)
    gt_own[...] = gsum.astype(BF16)
    gt[:, my_lanes] = gt_own[...]
    far_lanes = pl.ds(pl.multiple_of(256 + c * 128, 128), 128)

    ga_copies = [
        rcopy(gt_own, gt.at[:, my_lanes], ga_s.at[0], ga_r.at[0], sib),
        rcopy(
            gt_own, gt.at[:, far_lanes], ga_s.at[1], ga_r.at[1 + c],
            ((1 - xh) * 2, pqry, z),
        ),
        rcopy(
            gt_own, gt.at[:, far_lanes], ga_s.at[2], ga_r.at[1 + c],
            ((1 - xh) * 2 + 1, pqry, z),
        ),
    ]
    for copy in ga_copies:
        copy.start()

    for s in range(8):
        pa_arrival = rcopy(
            za.at[pl.ds(s * EI, EI), pl.ds(0, 256)],
            za.at[pl.ds(s * EI, EI), pl.ds(256, 256)],
            pa_s.at[s],
            pa_r.at[s],
            sib,
        )
        pa_arrival.wait_recv()
    rcopy(gt_own, gt.at[:, sib_lanes], ga_s.at[0], ga_r.at[0], sib).wait_recv()
    for n in range(2):
        lanes = pl.ds(256 + 128 * n, 128)
        rcopy(gt_own, gt.at[:, lanes], ga_s.at[1], ga_r.at[1 + n], sib).wait_recv()

    for q in range(8):
        weighted = dot(pan[q], za[...])
        row = jnp.sum(weighted * gt[...].astype(F32), axis=0, keepdims=True)
        for g in range(4):
            stage[q // 2, g, q % 2 : q % 2 + 1, :] = row[:, 128 * g : 128 * g + 128]

    def sc_copy(k, g):
        if g < 2:
            to_tok, frm = xh * 2 + g, qry
        else:
            to_tok, frm = (1 - xh) * 2 + g - 2, pqry
        return (
            rcopy(
                stage.at[k, g],
                srecv.at[c, frm],
                sc_s.at[k, g],
                sc_r.at[c, frm],
                (to_tok, xh * 4 + k, z),
            ),
            (to_tok == tok) & (xh * 4 + k == qry),
        )

    for k in range(4):
        for g in range(4):
            copy, here = sc_copy(k, g)
            if g < 2:

                @pl.when(here)
                def _():
                    srecv[c, qry] = stage[k, g]

                @pl.when(jnp.logical_not(here))
                def _():
                    copy.start()

            else:
                copy.start()

    for n in range(2):
        for f in range(NF):

            @pl.when(jnp.logical_not((c == n) & (qry == f) & (xh == xl)))
            def _():
                rcopy(
                    stage.at[0, 0], srecv.at[n, f], sc_s.at[0, 0], sc_r.at[n, f], sib
                ).wait_recv()

    factor = 1.0 / jnp.sqrt(F32(LQ * DOUT * DIN))
    for f in range(NF):
        fsum[2 * f : 2 * f + 2, :] = (srecv[0, f, 0:2, :] + srecv[1, f, 0:2, :]) * factor

    def fz_copy(dz):
        return rcopy(
            fsum, frecv.at[dz], fz_s.at[dz], fz_r.at[dz], (tok, qry, (z + dz) % NZ)
        )

    for dz in range(1, NZ):
        fz_copy(dz).start()
    for dz in range(1, NZ):
        fz_copy(dz).wait_recv()
    scores = fsum[...]
    for dz in range(1, NZ):
        scores = scores + frecv[dz]
    for f in range(NF):
        out_ref[:, SUB * f : SUB * f + SUB] = scores[2 * f : 2 * f + 2, 0:SUB]

    for k in range(1, NF):
        q_copy(k).wait_send()
        a_copy(k).wait_send()
        g_copy(k).wait_send()
    for dt in range(1, NT):
        t_copy(dt).wait_send()
    ev_far().wait_send()

    @pl.when(c != xh)
    def _():
        ev_near().wait_send()

    for dc, k in peers:
        qg_copy(dc, k).wait_send()

    @pl.when(jnp.logical_not(owner))
    def _():
        sib_copy().wait_send()

    for dz in range(1, NZ):
        fz_copy(dz).wait_send()
    zs_copy.wait_send()
    gather_close(zq, rq_s, rq_r)
    gather_close(za, ra_s, ra_r)
    for s in range(8):
        pa_copy(s).wait_send()
    for copy in ga_copies:
        copy.wait_send()
    for k in range(4):
        for g in range(4):
            copy, here = sc_copy(k, g)
            if g < 2:

                @pl.when(jnp.logical_not(here))
                def _():
                    copy.wait_send()

            else:
                copy.wait_send()


def shards(train_acts, train_grads, query_acts, query_grads, in_basis, out_basis, eigenvalues):
    dma = pltpu.SemaphoreType.DMA
    vm = pltpu.VMEM
    out = pl.pallas_call(
        kernel,
        out_shape=jax.ShapeDtypeStruct((2, ROWS), F32),
        in_specs=[pl.BlockSpec(memory_space=pl.ANY)] * 7,
        out_specs=pl.BlockSpec(memory_space=pltpu.VMEM),
        scratch_shapes=[
            vm((FI, ROWS), BF16), vm((FO, ROWS), BF16), vm((128, FI), BF16),
            vm((128, FO), BF16), vm((EI, FI), BF16), vm((EO, FO), BF16),
            vm((EO, 640), F32),
            vm((QP, 128), F32), vm((NF, QROWS, 128), F32), vm((2, QP, 128), BF16),
            vm((NF, EI, 128), BF16), vm((NF, EI, 128), BF16), vm((EI, 128), BF16),
            vm((NF, EO, 128), BF16), vm((NF, EO, 128), BF16),
            vm((EO, 128), BF16), vm((EO, 512), BF16),
            vm((EO, 640), BF16), vm((2, EO, 640), BF16), vm((EO, HALF), F32),
            vm((HALF, 512), BF16), vm((HALF, 256), BF16), vm((8, EO, HALF), BF16),
            vm((8, 128), F32), vm((NT, 8, 128), F32),
            vm((8, 128), F32), vm((8, 128), F32),
            vm((4, 4, 8, 128), F32), vm((2, NF, 8, 128), F32),
            vm((16, 128), F32), vm((NZ, 16, 128), F32),
            dma((7,)),
            dma((NF,)), dma((NF,)), dma((2, NF)), dma((2, NF)),
            dma((NF,)), dma((NF,)), dma((NF,)), dma((NF,)),
            dma((1,)), dma((1,)), dma((3,)), dma((3,)),
            dma((2,)), dma((2,)), dma((NT,)), dma((NT,)), dma((1,)), dma((1,)),
            dma((4, 8)), dma((8,)), dma((4, 8)), dma((8,)),
            dma((8,)), dma((8,)), dma((4, 4)), dma((2, NF)), dma((NZ,)), dma((NZ,)),
        ],
        compiler_params=pltpu.CompilerParams(
            collective_id=0, has_side_effects=True, vmem_limit_bytes=56 * 1024 * 1024
        ),
    )(
        train_acts.T,
        train_grads.T,
        query_acts.reshape(16 * LQ, FI),
        query_grads.reshape(16 * LQ, FO),
        in_basis.T,
        out_basis.T,
        eigenvalues,
    )
    return out.T


def solution(mesh):
    placed = (
        P("tok", "qry"),
        P("tok", "qry"),
        P(None, None, "qry"),
        P(None, None, "qry"),
        P("qry", "eig"),
        P("qry", "eig"),
        P("eig", "tok"),
    )
    return jax.shard_map(
        shards, mesh=mesh, in_specs=placed, out_specs=P("tok", "qry"), check_vma=False
    )
```
